32 devices in a mesh: groups: 2 (over x), tensor: 16 (over z, y, core).
Axes of the slice: x: 2, y: 2, z: 4, core: 2. Of those that a mesh axis runs over, the one named last changes fastest.
Arguments:
- queries: bfloat16 [512, 128, 128], P('groups', 'tensor'), parts along dimension 0, may hold values from -4.5 to 4.5
- node_keys: bfloat16 [8, 512, 128], P(None, ('groups', 'tensor')), parts along dimension 1, may hold values from -4.5 to 4.5
- node_values: bfloat16 [8, 512, 128], P(None, ('groups', 'tensor')), parts along dimension 1, may hold values from -15 to 15
- cache_keys: bfloat16 [8, 8192, 128], P(None, ('groups', 'tensor')), parts along dimension 1, may hold values from -4.5 to 4.5
- cache_values: bfloat16 [8, 8192, 128], P(None, ('groups', 'tensor')), parts along dimension 1, may hold values from -15 to 15
- parents: int32 [512], P('groups'), parts along dimension 0, may hold values from -1 to 254, as said below
- out_weight: bfloat16 [16384, 16384], P('tensor'), may hold values from -3 to 3
- residual: bfloat16 [512, 16384], P(('groups', 'tensor')), parts along dimension 0, may hold values from -6 to 6
- norm_gain: bfloat16 [16384], replicated, may hold values from 0.25 to 1.75
Outputs:
- quant_values: bfloat16 [512, 16384], P('groups'), parts along dimension 0
- quant_scales: bfloat16 [512, 128], P('groups'), parts along dimension 0
The draws below stay inside these ranges and needn't reach their ends.
There are 2 independent parts, one for each index of `groups`. The reference program is written for one: setup_inputs(seed, part) draws one part's arguments, and reference() takes and returns one part's arrays. A program takes and returns all parts, laid end to end along the dimension named above; an argument that names none is the same for every part. Nothing has to cross between parts.
Inputs may be any that keep to these rules, and one draw needn't show every extreme that they name: parents[0] is -1 and every other node's parent lies among the 8 nodes before it; the last node's parent is the node before it.
All inputs are finite; a program needn't handle non-finite values. Where the reference program divides by a largest or mean magnitude, that divisor is 1e-20 or more.
Results may differ from the reference program's by a relative error of at most 0.015.
Values may be sent and summed in bfloat16 or wider, within the bound.
A program may use at most 192 MiB of HBM per device.

```python
import math
import jax
import jax.numpy as jnp
from jax import lax

D = 16384
HEADS = 128
HD = 128
KV_SLOTS = 8
BLK = 128
TOK = 256
CACHE = 4096
N_TENSOR = 16


def draw_queries(key, part):
    key = jax.random.fold_in(key, 1)
    base = jnp.clip(jax.random.normal(key, (TOK, HEADS, HD), jnp.float32), -4.5, 4.5)
    return base.astype(jnp.bfloat16)


def draw_cache_keys(key, part):
    key = jax.random.fold_in(key, 2)
    base = jnp.clip(jax.random.normal(key, (KV_SLOTS, CACHE, HD), jnp.float32), -4.5, 4.5)
    return base.astype(jnp.bfloat16)


def draw_parents(key, part):
    key = jax.random.fold_in(key, 3)
    index = jnp.arange(TOK, dtype=jnp.int32)
    bits = jax.random.randint(key, (TOK,), 0, 1048576)
    span = jnp.maximum(jnp.minimum(index, 8), 1)
    chosen = index - 1 - jnp.remainder(bits, span)
    chosen = jnp.where(index == 0, -1, chosen)
    chosen = jnp.where(index == TOK - 1, TOK - 2, chosen)
    return chosen.astype(jnp.int32)


def draw_residual(key, part):
    key = jax.random.fold_in(key, 4)
    keys = jax.random.split(key, 3)
    row_scale = jnp.exp(jax.random.uniform(keys[0], (TOK, 1), jnp.float32, 0.0, math.log(10.0)))
    col_scale = jnp.exp(jax.random.uniform(keys[1], (1, D), jnp.float32, 0.0, math.log(10.0)))
    trend = jnp.exp(math.log(3.0) * jnp.arange(D, dtype=jnp.float32)[None, :] / D)
    spread = 0.005 * row_scale * col_scale * trend
    base = jnp.clip(jax.random.normal(keys[2], (TOK, D), jnp.float32), -4.0, 4.0)
    return (spread * base).astype(jnp.bfloat16)


def draw_out_weight(key, part):
    key = jax.random.fold_in(key, 5)
    keys = jax.random.split(key, 2)
    pairing = jax.random.permutation(keys[0], N_TENSOR)
    row_block = jnp.arange(D, dtype=jnp.int32) // (D // N_TENSOR)
    col_block = jnp.arange(D, dtype=jnp.int32) // (D // N_TENSOR)
    spike = jnp.where(pairing[row_block][:, None] == col_block[None, :], 4.0, 1.0)
    rise = math.log(3.0)
    base = jnp.clip(jax.random.normal(keys[1], (D, D), jnp.float32), -4.0, 4.0)
    trend = jnp.exp(rise * jnp.arange(D, dtype=jnp.float32) / D)[None, :]
    return (base * spike * trend / math.sqrt(D)).astype(jnp.bfloat16)


def block_levels(own_key, dims, cuts, smallest, high):
    factor_of, own = 1.0, jax.random.fold_in(own_key, 6)
    for axis_at, blocks in cuts:
        draws = jnp.exp(jax.random.uniform(jax.random.fold_in(own, axis_at), (blocks,), jnp.float32, smallest / len(cuts), high / len(cuts)))
        factor_of = factor_of * jnp.repeat(draws, dims[axis_at] // blocks).reshape([-1 if axis == axis_at else 1 for axis in range(len(dims))])
    return factor_of


def bell_draw(stream_key, extent, deviation, bound, cuts=(), kind=jnp.bfloat16):
    factor_of = block_levels(stream_key, extent, cuts, -0.22, 0.18) if cuts else 1.0
    entries = jax.random.normal(stream_key, extent, jnp.float32) * deviation * factor_of
    return jnp.minimum(jnp.maximum(entries, -bound), bound).astype(kind)


def setup_inputs(seed: int = 0, part: int = 0) -> dict:
    key_of = jax.random.split(jax.random.key(seed), 10)
    part_splits = jax.random.split(jax.random.fold_in(key_of[9], part), 10)
    return {
        "queries": draw_queries(jax.random.fold_in(jax.random.fold_in(key_of[9], part), 71), part),
        "node_keys": bell_draw(part_splits[1], (KV_SLOTS, TOK, HD), 1.0, 4.5, ((1, 16),)),
        "node_values": bell_draw(part_splits[2], (KV_SLOTS, TOK, HD), 3.0, 15.0, ((1, 16),)),
        "cache_keys": draw_cache_keys(jax.random.fold_in(jax.random.fold_in(key_of[9], part), 71), part),
        "cache_values": bell_draw(part_splits[4], (KV_SLOTS, CACHE, HD), 3.0, 15.0, ((1, 16),)),
        "parents": draw_parents(jax.random.fold_in(jax.random.fold_in(key_of[9], part), 71), part),
        "out_weight": draw_out_weight(jax.random.fold_in(key_of[9], 71), part),
        "residual": draw_residual(jax.random.fold_in(jax.random.fold_in(key_of[9], part), 71), part),
        "norm_gain": jnp.clip(1.0 + 0.15 * jax.random.normal(key_of[8], (D,), jnp.float32), 0.25, 1.75).astype(jnp.bfloat16),
    }


def hadamard(size):
    rows = jnp.arange(size, dtype=jnp.int32)
    parity = jnp.zeros((size, size), jnp.int32)
    bit = 1
    while bit < size:
        left = (jnp.bitwise_and(rows, bit) > 0).astype(jnp.int32)
        parity = parity + left[:, None] * left[None, :]
        bit = bit * 2
    signs = 1 - 2 * jnp.remainder(parity, 2)
    return signs.astype(jnp.float32) / math.sqrt(size)

def rotate(values, table):
    shape = values.shape
    flat = values.reshape(-1, table.shape[0])
    return jnp.dot(flat, table, precision=lax.Precision.HIGHEST).reshape(shape)

def quantize(values, block):
    count, width = values.shape
    grouped = values.reshape(count, width // block, block)
    scales = (lax.optimization_barrier(jnp.max(jnp.abs(grouped), axis=-1)) + 1e-06).astype(jnp.bfloat16)
    levels = (grouped / scales.astype(jnp.float32)[..., None]).astype(jnp.bfloat16)
    return (levels.reshape(count, width), scales)

def ancestors(parents):
    count = parents.shape[0]
    index = jnp.arange(count, dtype=jnp.int32)
    reach = ((index[None, :] == index[:, None]) | (index[None, :] == parents[:, None])).astype(jnp.float32)
    for step in range(max(1, (count - 1).bit_length())):
        reach = jnp.minimum(jnp.dot(reach, reach, precision=lax.Precision.HIGHEST), 1.0)
    return reach > 0.5

def reference(queries, node_keys, node_values, cache_keys, cache_values, parents, out_weight, residual, norm_gain):
    visible = ancestors(parents)
    group = HEADS // KV_SLOTS
    allowed = jnp.concatenate([jnp.ones((TOK, CACHE), bool), visible], 1)[:, None, :]

    def one_slot(slot):
        query = lax.dynamic_slice_in_dim(queries, slot * group, group, 1).astype(jnp.float32)
        keys = jnp.concatenate([cache_keys[slot], node_keys[slot]], 0).astype(jnp.float32)
        values = jnp.concatenate([cache_values[slot], node_values[slot]], 0).astype(jnp.float32)
        scores = jnp.einsum('thd,kd->thk', query, keys) / math.sqrt(HD)
        scores = jnp.where(allowed, scores, -1e+30)
        top = lax.optimization_barrier(jnp.max(scores, -1, keepdims=True))
        exp_scores = jnp.where(allowed, jnp.exp(scores - top), 0.0)
        totals = lax.optimization_barrier(jnp.sum(exp_scores, -1, keepdims=True))
        weights = exp_scores.astype(jnp.bfloat16).astype(jnp.float32)
        return (jnp.einsum('thk,kd->thd', weights, values) / totals).astype(jnp.bfloat16)
    slots = jnp.arange(KV_SLOTS, dtype=jnp.int32)
    heads_out = lax.map(one_slot, slots)
    attended = jnp.transpose(heads_out, (1, 0, 2, 3)).reshape(TOK, D)
    rows = HEADS // N_TENSOR * HD

    def add_range(total, index):
        piece = lax.dynamic_slice_in_dim(attended, index * rows, rows, 1)
        weight = lax.dynamic_slice_in_dim(out_weight, index * rows, rows, 0)
        partial_value = jnp.dot(piece, weight, preferred_element_type=jnp.float32)
        rounded = lax.optimization_barrier(partial_value.astype(jnp.bfloat16))
        return (total + rounded.astype(jnp.float32), None)
    ranges = jnp.arange(N_TENSOR, dtype=jnp.int32)
    projected, unused = lax.scan(add_range, jnp.zeros((TOK, D), jnp.float32), ranges)
    state = residual.astype(jnp.float32) + projected
    normed = state * lax.rsqrt(lax.optimization_barrier(jnp.mean(state * state, -1, keepdims=True)) + 1e-05) * norm_gain.astype(jnp.float32)
    rotated = rotate(normed, hadamard(BLK))
    quant_values, quant_scales = quantize(rotated, BLK)
    return (quant_values, quant_scales)
```

```python
import functools
import math

import jax
import jax.numpy as jnp
import ml_dtypes
import numpy as np
from jax import lax
from jax.experimental import pallas as pl
from jax.experimental.pallas import tpu as pltpu
from jax.sharding import PartitionSpec as P

BLK = 128
MESH = pl.DeviceIdType.MESH


def signs(size):
    index = np.arange(size)
    both = index[:, None] & index[None, :]
    parity = np.zeros((size, size), np.int64)
    while both.any():
        parity ^= both & 1
        both = both >> 1
    return (1 - 2 * parity).astype(ml_dtypes.bfloat16)


def ring_chip(pos, chips):
    turn = chips // 2
    back = pos // turn
    return (1 - back) * (2 * pos) + back * (2 * (chips - 1 - pos) + 1)


def ring_pos(chip, chips):
    odd = chip % 2
    level = chip // 2
    return (1 - odd) * level + odd * (chips - 1 - level)


def send(src, dst, send_sem, recv_sem, target):
    return pltpu.make_async_remote_copy(
        src_ref=src,
        dst_ref=dst,
        send_sem=send_sem,
        recv_sem=recv_sem,
        device_id={"tensor": target},
        device_id_type=MESH,
    )


def greet(targets):
    barrier = pltpu.get_barrier_semaphore()
    for target in targets:
        pl.semaphore_signal(barrier, inc=1, device_id={"tensor": target}, device_id_type=MESH)
    pl.semaphore_wait(barrier, len(targets))


def project_kernel(
    devices,
    att_ref,
    weight_ref,
    residual_ref,
    gain_ref,
    table_ref,
    out_ref,
    wbuf,
    pair_out,
    pair_in,
    part,
    ring_out,
    ring_in,
    swap_out,
    swap_in,
    mine,
    state,
    packed,
    w_sem,
    pair_send,
    pair_recv,
    ring_send,
    ring_recv,
    swap_send,
    swap_recv,
    keep_sem,
    far_send,
    far_recv,
    near_send,
    near_recv,
):
    chips = devices // 2
    own, width = state.shape
    rows = 2 * own
    half_width = width // 2
    lane = half_width // 4
    tile = wbuf.shape[2]
    per = half_width // (2 * tile)
    total = 4 * per
    me = lax.axis_index("tensor")
    core = me % 2
    chip = me // 2
    pos = ring_pos(chip, chips)
    right = 2 * ring_chip((pos + 1) % chips, chips) + core
    left = 2 * ring_chip((pos + chips - 1) % chips, chips) + core
    pair = 2 * chip + 1 - core

    def fetch(step):
        phase = step // per
        side = (core + 1 + phase % 2) % 2
        column = side * half_width + ((phase // 2) * per + step % per) * tile
        return pltpu.make_async_copy(
            weight_ref.at[:, pl.ds(pl.multiple_of(column, tile), tile)],
            wbuf.at[step % 3],
            w_sem.at[step % 3],
        )

    fetch(0).start()
    fetch(1).start()
    greet((pair, left, right))

    def product(step):
        fetch(step).wait()

        @pl.when(step + 2 < total)
        def _():
            fetch(step + 2).start()

        return jnp.dot(att_ref[...], wbuf[step % 3], preferred_element_type=jnp.float32)

    def pair_copy(index):
        return send(
            pair_out.at[index], pair_in.at[index], pair_send.at[index], pair_recv.at[index], pair
        )

    def give(half):
        def body(i, carry):
            index = half * per + i
            pair_out[index] = product(2 * half * per + i).astype(jnp.bfloat16)
            pair_copy(index).start()
            return carry

        lax.fori_loop(0, per, body, 0)

    def keep(half):
        def body(i, carry):
            index = half * per + i
            own_part = product((2 * half + 1) * per + i)
            pair_copy(index).wait_recv()
            part[:, pl.ds(pl.multiple_of(index * tile, tile), tile)] = own_part + pair_in[
                index
            ].astype(jnp.float32)
            return carry

        lax.fori_loop(0, per, body, 0)

    def ring_copy(stream, step):
        return send(
            ring_out.at[stream, step],
            ring_in.at[stream, step],
            ring_send.at[stream, step],
            ring_recv.at[stream, step],
            left if stream % 2 else right,
        )

    def ring_step(stream, step, first):
        if stream % 2:
            target = (pos + 1 + step) % chips
        else:
            target = (pos + chips - 1 - step) % chips
        row = pl.multiple_of(ring_chip(target, chips) * rows, rows)
        value = part[pl.ds(row, rows), stream * lane : (stream + 1) * lane]
        if not first:
            ring_copy(stream, step - 1).wait_recv()
            value = value + ring_in[stream, step - 1].astype(jnp.float32)
        ring_out[stream, step] = value.astype(jnp.bfloat16)
        ring_copy(stream, step).start()

    give(0)
    keep(0)
    ring_step(0, 0, True)
    ring_step(1, 0, True)
    give(1)
    ring_step(0, 1, False)
    ring_step(1, 1, False)
    keep(1)
    ring_step(2, 0, True)
    ring_step(3, 0, True)

    def around(step, carry):
        for stream in (0, 1):
            ring_step(stream, step, False)
        for stream in (2, 3):
            ring_step(stream, step - 1, False)
        return carry

    lax.fori_loop(2, chips - 1, around, 0)
    for stream in (2, 3):
        ring_step(stream, chips - 2, False)
    row = pl.multiple_of(chip * rows, rows)
    for stream in range(4):
        ring_copy(stream, chips - 2).wait_recv()
        columns = slice(stream * lane, (stream + 1) * lane)
        mine[:, columns] = part[pl.ds(row, rows), columns] + ring_in[stream, chips - 2].astype(
            jnp.float32
        )
    swap_out[...] = mine[pl.ds(pl.multiple_of((1 - core) * own, own), own), :]
    swap = send(swap_out, swap_in, swap_send, swap_recv, pair)
    swap.start()
    state[:, pl.ds(pl.multiple_of(core * half_width, half_width), half_width)] = mine[
        pl.ds(pl.multiple_of(core * own, own), own), :
    ]
    swap.wait_recv()
    state[:, pl.ds(pl.multiple_of((1 - core) * half_width, half_width), half_width)] = swap_in[...]

    group = 8
    step_width = group * BLK

    def squares(i, acc):
        columns = pl.ds(pl.multiple_of(i * step_width, step_width), step_width)
        value = state[:, columns] + residual_ref[:, columns].astype(jnp.float32)
        state[:, columns] = value
        return acc + value * value

    acc = lax.fori_loop(
        0, width // step_width, squares, jnp.zeros((own, step_width), jnp.float32)
    )
    inverse = lax.rsqrt(jnp.sum(acc, axis=1, keepdims=True) / width + 1e-05)
    table = table_ref[...]
    lanes = lax.broadcasted_iota(jnp.int32, (own, width // BLK), 1)

    def rotate_group(i, scales):
        blocks = []
        for b in range(group):
            columns = pl.ds(pl.multiple_of(i * step_width + b * BLK, BLK), BLK)
            blocks.append(
                state[:, columns] * inverse * gain_ref[:, columns].astype(jnp.float32)
            )
        normed = jnp.concatenate(blocks, axis=0)
        high = normed.astype(jnp.bfloat16)
        low = (normed - high.astype(jnp.float32)).astype(jnp.bfloat16)
        rotated = (
            jnp.dot(high, table, preferred_element_type=jnp.float32)
            + jnp.dot(low, table, preferred_element_type=jnp.float32)
        ) * (1.0 / math.sqrt(BLK))
        scale = (
            (jnp.max(jnp.abs(rotated), axis=1, keepdims=True) + 1e-06)
            .astype(jnp.bfloat16)
            .astype(jnp.float32)
        )
        levels = (rotated / scale).astype(jnp.bfloat16)
        for b in range(group):
            columns = pl.ds(pl.multiple_of(i * step_width + b * BLK, BLK), BLK)
            packed[:, columns] = levels[b * own : (b + 1) * own, :]
            scales = jnp.where(lanes == i * group + b, scale[b * own : (b + 1) * own, :], scales)
        return scales

    scales = lax.fori_loop(
        0, width // step_width, rotate_group, jnp.zeros((own, width // BLK), jnp.float32)
    )
    packed[:, width:] = scales.astype(jnp.bfloat16)

    full = packed.shape[1]
    cut = (full // 2 // BLK) * BLK
    pieces = (pl.ds(0, cut), pl.ds(cut, full - cut))
    hops = chips // 2

    def owner(d, hop):
        where = (pos + hop) % chips if d else (pos + chips - hop) % chips
        return 2 * ring_chip(where, chips) + core

    def far_copy(d, hop, piece):
        block = owner(d, hop - 1)
        dst = out_ref.at[block, :, pieces[piece]]
        src = packed.at[:, pieces[piece]] if hop == 1 else dst
        at = (d * hops + hop - 1) * 2 + piece
        return send(src, dst, far_send.at[at], far_recv.at[at], left if d else right)

    def near_copy(d, hop, piece):
        block = owner(d, hop)
        dst = out_ref.at[block, :, pieces[piece]]
        src = packed.at[:, pieces[piece]] if hop == 0 else dst
        at = (d * (hops + 1) + hop) * 2 + piece
        return send(src, dst, near_send.at[at], near_recv.at[at], pair)

    def goes(d, hop, piece):
        return hop < hops or piece == d

    order = ((0, 0), (1, 1), (0, 1), (1, 0))
    for d, piece in order:
        far_copy(d, 1, piece).start()
    own_copy = pltpu.make_async_copy(packed, out_ref.at[me], keep_sem)
    own_copy.start()
    for piece in (0, 1):
        near_copy(0, 0, piece).start()
    for hop in range(1, hops + 1):
        for d, piece in order:
            if goes(d, hop, piece):
                far_copy(d, hop, piece).wait_recv()
                if hop < hops and goes(d, hop + 1, piece):
                    far_copy(d, hop + 1, piece).start()
                near_copy(d, hop, piece).start()
    own_copy.wait()
    for piece in (0, 1):
        near_copy(0, 0, piece).wait()
    for hop in range(1, hops + 1):
        for d, piece in order:
            if goes(d, hop, piece):
                far_copy(d, hop, piece).wait_send()
                near_copy(d, hop, piece).wait()
    swap.wait_send()

    def drain_pair(i, carry):
        pair_copy(i).wait_send()
        return carry

    lax.fori_loop(0, 2 * per, drain_pair, 0)

    def drain_ring(step, carry):
        for stream in range(4):
            ring_copy(stream, step).wait_send()
        return carry

    lax.fori_loop(0, chips - 1, drain_ring, 0)


def project(devices, attended, out_weight, residual, norm_gain):
    tok_count, depth = attended.shape
    width = out_weight.shape[1]
    own = residual.shape[0]
    chips = devices // 2
    hops = chips // 2
    half_width = width // 2
    lane = half_width // 4
    tile = half_width // 8
    full = width + width // BLK
    bf16, f32 = jnp.bfloat16, jnp.float32
    dma = pltpu.SemaphoreType.DMA
    vmem = pl.BlockSpec(memory_space=pltpu.VMEM)
    hbm = pl.BlockSpec(memory_space=pl.ANY)
    return pl.pallas_call(
        functools.partial(project_kernel, devices),
        out_shape=jax.ShapeDtypeStruct((devices, own, full), bf16),
        in_specs=[vmem, hbm, vmem, vmem, vmem],
        out_specs=hbm,
        scratch_shapes=[
            pltpu.VMEM((3, depth, tile), bf16),
            pltpu.VMEM((8, tok_count, tile), bf16),
            pltpu.VMEM((8, tok_count, tile), bf16),
            pltpu.VMEM((tok_count, half_width), f32),
            pltpu.VMEM((4, chips - 1, 2 * own, lane), bf16),
            pltpu.VMEM((4, chips - 1, 2 * own, lane), bf16),
            pltpu.VMEM((own, half_width), f32),
            pltpu.VMEM((own, half_width), f32),
            pltpu.VMEM((2 * own, half_width), f32),
            pltpu.VMEM((own, width), f32),
            pltpu.VMEM((own, full), bf16),
            dma((3,)),
            dma((8,)),
            dma((8,)),
            dma((4, chips - 1)),
            dma((4, chips - 1)),
            dma,
            dma,
            dma,
            dma((4 * hops,)),
            dma((4 * hops,)),
            dma((4 * (hops + 1),)),
            dma((4 * (hops + 1),)),
        ],
        compiler_params=pltpu.CompilerParams(
            collective_id=0, has_side_effects=True, vmem_limit_bytes=52 * 1024 * 1024
        ),
        cost_estimate=pl.CostEstimate(
            flops=2 * tok_count * depth * width,
            bytes_accessed=2 * depth * width,
            transcendentals=0,
        ),
    )(attended, out_weight, residual, norm_gain.reshape(1, -1), jnp.asarray(signs(BLK)))


def ancestors(parents):
    count = parents.shape[0]
    index = jnp.arange(count, dtype=jnp.int32)
    reach = ((index[None, :] == index[:, None]) | (index[None, :] == parents[:, None])).astype(
        jnp.float32
    )
    for step in range(max(1, (count - 1).bit_length())):
        reach = jnp.minimum(jnp.dot(reach, reach, precision=lax.Precision.HIGHEST), 1.0)
    return reach > 0.5


def shards(
    queries,
    node_keys,
    node_values,
    cache_keys,
    cache_values,
    parents,
    out_weight,
    residual,
    norm_gain,
):
    tok_count, group, head_size = queries.shape
    devices = lax.axis_size("tensor")
    copies = devices // cache_keys.shape[0]
    prefix_keys = jnp.repeat(cache_keys, copies, 0)
    prefix_values = jnp.repeat(cache_values, copies, 0)
    branch_keys = jnp.repeat(node_keys, copies, 0)
    branch_values = jnp.repeat(node_values, copies, 0)
    past_keys, past_values, tree_keys, tree_values = (
        lax.all_to_all(prefix_keys, "tensor", split_axis=0, concat_axis=1, tiled=True),
        lax.all_to_all(prefix_values, "tensor", split_axis=0, concat_axis=1, tiled=True),
        lax.all_to_all(branch_keys, "tensor", split_axis=0, concat_axis=1, tiled=True),
        lax.all_to_all(branch_values, "tensor", split_axis=0, concat_axis=1, tiled=True),
    )
    cache_length = past_keys.shape[1]
    visible = ancestors(parents)
    allowed = jnp.concatenate([jnp.ones((tok_count, cache_length), bool), visible], 1)[:, None, :]
    keys = jnp.concatenate([past_keys[0], tree_keys[0]], 0)
    values = jnp.concatenate([past_values[0], tree_values[0]], 0)
    scores = jnp.einsum(
        "thd,kd->thk", queries, keys, preferred_element_type=jnp.float32
    ) / math.sqrt(head_size)
    scores = jnp.where(allowed, scores, -1e30)
    top = jnp.max(scores, -1, keepdims=True)
    exp_scores = jnp.where(allowed, jnp.exp(scores - top), 0.0)
    totals = jnp.sum(exp_scores, -1, keepdims=True)
    weights = exp_scores.astype(jnp.bfloat16)
    mixed = jnp.einsum("thk,kd->thd", weights, values, preferred_element_type=jnp.float32) / totals
    attended = mixed.astype(jnp.bfloat16).reshape(tok_count, group * head_size)
    gathered = project(devices, attended, out_weight, residual, norm_gain)
    width = out_weight.shape[1]
    return (
        gathered[:, :, :width].reshape(tok_count, width),
        gathered[:, :, width:].reshape(tok_count, width // BLK),
    )


def solution(mesh):
    in_specs = (
        P("groups", "tensor", None),
        P(None, ("groups", "tensor"), None),
        P(None, ("groups", "tensor"), None),
        P(None, ("groups", "tensor"), None),
        P(None, ("groups", "tensor"), None),
        P("groups"),
        P("tensor", None),
        P(("groups", "tensor"), None),
        P(),
    )
    out_specs = (P("groups", None), P("groups", None))
    return jax.shard_map(shards, mesh=mesh, in_specs=in_specs, out_specs=out_specs, check_vma=False)
```

```python
import functools
import math

import jax
import jax.numpy as jnp
import ml_dtypes
import numpy as np
from jax import lax
from jax.experimental import pallas as pl
from jax.experimental.pallas import tpu as pltpu
from jax.sharding import PartitionSpec as P

BLK = 128
MESH = pl.DeviceIdType.MESH


def signs(size):
    index = np.arange(size)
    both = index[:, None] & index[None, :]
    parity = np.zeros((size, size), np.int64)
    while both.any():
        parity ^= both & 1
        both = both >> 1
    return (1 - 2 * parity).astype(ml_dtypes.bfloat16)


def ring_chip(pos, chips):
    turn = chips // 2
    back = pos // turn
    return (1 - back) * (2 * pos) + back * (2 * (chips - 1 - pos) + 1)


def ring_pos(chip, chips):
    odd = chip % 2
    level = chip // 2
    return (1 - odd) * level + odd * (chips - 1 - level)


def send(src, dst, send_sem, recv_sem, target):
    return pltpu.make_async_remote_copy(
        src_ref=src,
        dst_ref=dst,
        send_sem=send_sem,
        recv_sem=recv_sem,
        device_id={"tensor": target},
        device_id_type=MESH,
    )


def greet(targets):
    barrier = pltpu.get_barrier_semaphore()
    for target in targets:
        pl.semaphore_signal(barrier, inc=1, device_id={"tensor": target}, device_id_type=MESH)
    pl.semaphore_wait(barrier, len(targets))


def project_kernel(
    devices,
    att_ref,
    weight_ref,
    residual_ref,
    gain_ref,
    table_ref,
    out_ref,
    wbuf,
    pair_out,
    pair_in,
    part,
    ring_out,
    ring_in,
    swap_out,
    swap_in,
    mine,
    state,
    packed,
    w_sem,
    pair_send,
    pair_recv,
    ring_send,
    ring_recv,
    swap_send,
    swap_recv,
    keep_sem,
    far_send,
    far_recv,
    near_send,
    near_recv,
):
    chips = devices // 2
    own, width = state.shape
    rows = 2 * own
    half_width = width // 2
    lane = half_width // 4
    tile = wbuf.shape[2]
    per = half_width // (2 * tile)
    total = 4 * per
    me = lax.axis_index("tensor")
    core = me % 2
    chip = me // 2
    pos = ring_pos(chip, chips)
    right = 2 * ring_chip((pos + 1) % chips, chips) + core
    left = 2 * ring_chip((pos + chips - 1) % chips, chips) + core
    pair = 2 * chip + 1 - core

    def fetch(step):
        phase = step // per
        side = (core + 1 + phase % 2) % 2
        column = side * half_width + ((phase // 2) * per + step % per) * tile
        return pltpu.make_async_copy(
            weight_ref.at[:, pl.ds(pl.multiple_of(column, tile), tile)],
            wbuf.at[step % 3],
            w_sem.at[step % 3],
        )

    fetch(0).start()
    fetch(1).start()
    greet((pair, left, right))

    def product(step):
        fetch(step).wait()

        @pl.when(step + 2 < total)
        def _():
            fetch(step + 2).start()

        return jnp.dot(att_ref[...], wbuf[step % 3], preferred_element_type=jnp.float32)

    def pair_copy(index):
        return send(
            pair_out.at[index], pair_in.at[index], pair_send.at[index], pair_recv.at[index], pair
        )

    def give(half):
        def body(i, carry):
            index = half * per + i
            pair_out[index] = product(2 * half * per + i).astype(jnp.bfloat16)
            pair_copy(index).start()
            return carry

        lax.fori_loop(0, per, body, 0)

    def keep(half):
        def body(i, carry):
            index = half * per + i
            own_part = product((2 * half + 1) * per + i)
            pair_copy(index).wait_recv()
            part[:, pl.ds(pl.multiple_of(index * tile, tile), tile)] = own_part + pair_in[
                index
            ].astype(jnp.float32)
            return carry

        lax.fori_loop(0, per, body, 0)

    def ring_copy(stream, step):
        return send(
            ring_out.at[stream, step],
            ring_in.at[stream, step],
            ring_send.at[stream, step],
            ring_recv.at[stream, step],
            left if stream % 2 else right,
        )

    def ring_step(stream, step, first):
        if stream % 2:
            target = (pos + 1 + step) % chips
        else:
            target = (pos + chips - 1 - step) % chips
        row = pl.multiple_of(ring_chip(target, chips) * rows, rows)
        value = part[pl.ds(row, rows), stream * lane : (stream + 1) * lane]
        if not first:
            ring_copy(stream, step - 1).wait_recv()
            value = value + ring_in[stream, step - 1].astype(jnp.float32)
        ring_out[stream, step] = value.astype(jnp.bfloat16)
        ring_copy(stream, step).start()

    give(0)
    keep(0)
    ring_step(0, 0, True)
    ring_step(1, 0, True)
    give(1)
    ring_step(0, 1, False)
    ring_step(1, 1, False)
    keep(1)
    ring_step(2, 0, True)
    ring_step(3, 0, True)

    def around(step, carry):
        for stream in (0, 1):
            ring_step(stream, step, False)
        for stream in (2, 3):
            ring_step(stream, step - 1, False)
        return carry

    lax.fori_loop(2, chips - 1, around, 0)
    for stream in (2, 3):
        ring_step(stream, chips - 2, False)
    row = pl.multiple_of(chip * rows, rows)
    for stream in range(4):
        ring_copy(stream, chips - 2).wait_recv()
        columns = slice(stream * lane, (stream + 1) * lane)
        mine[:, columns] = part[pl.ds(row, rows), columns] + ring_in[stream, chips - 2].astype(
            jnp.float32
        )
    swap_out[...] = mine[pl.ds(pl.multiple_of((1 - core) * own, own), own), :]
    swap = send(swap_out, swap_in, swap_send, swap_recv, pair)
    swap.start()
    state[:, pl.ds(pl.multiple_of(core * half_width, half_width), half_width)] = mine[
        pl.ds(pl.multiple_of(core * own, own), own), :
    ]
    swap.wait_recv()
    state[:, pl.ds(pl.multiple_of((1 - core) * half_width, half_width), half_width)] = swap_in[...]

    group = 8
    step_width = group * BLK

    def squares(i, acc):
        columns = pl.ds(pl.multiple_of(i * step_width, step_width), step_width)
        value = state[:, columns] + residual_ref[:, columns].astype(jnp.float32)
        state[:, columns] = value
        return acc + value * value

    acc = lax.fori_loop(
        0, width // step_width, squares, jnp.zeros((own, step_width), jnp.float32)
    )
    inverse = lax.rsqrt(jnp.sum(acc, axis=1, keepdims=True) / width + 1e-05)
    table = table_ref[...]
    lanes = lax.broadcasted_iota(jnp.int32, (own, width // BLK), 1)

    def rotate_group(i, scales):
        blocks = []
        for b in range(group):
            columns = pl.ds(pl.multiple_of(i * step_width + b * BLK, BLK), BLK)
            blocks.append(
                state[:, columns] * inverse * gain_ref[:, columns].astype(jnp.float32)
            )
        normed = jnp.concatenate(blocks, axis=0)
        high = normed.astype(jnp.bfloat16)
        low = (normed - high.astype(jnp.float32)).astype(jnp.bfloat16)
        rotated = (
            jnp.dot(high, table, preferred_element_type=jnp.float32)
            + jnp.dot(low, table, preferred_element_type=jnp.float32)
        ) * (1.0 / math.sqrt(BLK))
        scale = (
            (jnp.max(jnp.abs(rotated), axis=1, keepdims=True) + 1e-06)
            .astype(jnp.bfloat16)
            .astype(jnp.float32)
        )
        levels = (rotated / scale).astype(jnp.bfloat16)
        for b in range(group):
            columns = pl.ds(pl.multiple_of(i * step_width + b * BLK, BLK), BLK)
            packed[:, columns] = levels[b * own : (b + 1) * own, :]
            scales = jnp.where(lanes == i * group + b, scale[b * own : (b + 1) * own, :], scales)
        return scales

    scales = lax.fori_loop(
        0, width // step_width, rotate_group, jnp.zeros((own, width // BLK), jnp.float32)
    )
    packed[:, width:] = scales.astype(jnp.bfloat16)

    full = packed.shape[1]
    cut = (full // 2 // BLK) * BLK
    pieces = (pl.ds(0, cut), pl.ds(cut, full - cut))
    hops = chips // 2

    def owner(d, hop):
        where = (pos + hop) % chips if d else (pos + chips - hop) % chips
        return 2 * ring_chip(where, chips) + core

    def far_copy(d, hop, piece):
        block = owner(d, hop - 1)
        dst = out_ref.at[block, :, pieces[piece]]
        src = packed.at[:, pieces[piece]] if hop == 1 else dst
        at = (d * hops + hop - 1) * 2 + piece
        return send(src, dst, far_send.at[at], far_recv.at[at], left if d else right)

    def near_copy(d, hop, piece):
        block = owner(d, hop)
        dst = out_ref.at[block, :, pieces[piece]]
        src = packed.at[:, pieces[piece]] if hop == 0 else dst
        at = (d * (hops + 1) + hop) * 2 + piece
        return send(src, dst, near_send.at[at], near_recv.at[at], pair)

    def goes(d, hop, piece):
        return hop < hops or piece == d

    order = ((0, 0), (1, 1), (0, 1), (1, 0))
    for d, piece in order:
        far_copy(d, 1, piece).start()
    own_copy = pltpu.make_async_copy(packed, out_ref.at[me], keep_sem)
    own_copy.start()
    for piece in (0, 1):
        near_copy(0, 0, piece).start()
    for hop in range(1, hops + 1):
        for d, piece in order:
            if goes(d, hop, piece):
                far_copy(d, hop, piece).wait_recv()
                if hop < hops and goes(d, hop + 1, piece):
                    far_copy(d, hop + 1, piece).start()
                near_copy(d, hop, piece).start()
    own_copy.wait()
    for piece in (0, 1):
        near_copy(0, 0, piece).wait()
    for hop in range(1, hops + 1):
        for d, piece in order:
            if goes(d, hop, piece):
                far_copy(d, hop, piece).wait_send()
                near_copy(d, hop, piece).wait()
    swap.wait_send()

    def drain_pair(i, carry):
        pair_copy(i).wait_send()
        return carry

    lax.fori_loop(0, 2 * per, drain_pair, 0)

    def drain_ring(step, carry):
        for stream in range(4):
            ring_copy(stream, step).wait_send()
        return carry

    lax.fori_loop(0, chips - 1, drain_ring, 0)


def project(devices, attended, out_weight, residual, norm_gain):
    tok_count, depth = attended.shape
    width = out_weight.shape[1]
    own = residual.shape[0]
    chips = devices // 2
    hops = chips // 2
    half_width = width // 2
    lane = half_width // 4
    tile = half_width // 8
    full = width + width // BLK
    bf16, f32 = jnp.bfloat16, jnp.float32
    dma = pltpu.SemaphoreType.DMA
    vmem = pl.BlockSpec(memory_space=pltpu.VMEM)
    hbm = pl.BlockSpec(memory_space=pl.ANY)
    return pl.pallas_call(
        functools.partial(project_kernel, devices),
        out_shape=jax.ShapeDtypeStruct((devices, own, full), bf16),
        in_specs=[vmem, hbm, vmem, vmem, vmem],
        out_specs=hbm,
        scratch_shapes=[
            pltpu.VMEM((3, depth, tile), bf16),
            pltpu.VMEM((8, tok_count, tile), bf16),
            pltpu.VMEM((8, tok_count, tile), bf16),
            pltpu.VMEM((tok_count, half_width), f32),
            pltpu.VMEM((4, chips - 1, 2 * own, lane), bf16),
            pltpu.VMEM((4, chips - 1, 2 * own, lane), bf16),
            pltpu.VMEM((own, half_width), f32),
            pltpu.VMEM((own, half_width), f32),
            pltpu.VMEM((2 * own, half_width), f32),
            pltpu.VMEM((own, width), f32),
            pltpu.VMEM((own, full), bf16),
            dma((3,)),
            dma((8,)),
            dma((8,)),
            dma((4, chips - 1)),
            dma((4, chips - 1)),
            dma,
            dma,
            dma,
            dma((4 * hops,)),
            dma((4 * hops,)),
            dma((4 * (hops + 1),)),
            dma((4 * (hops + 1),)),
        ],
        compiler_params=pltpu.CompilerParams(
            collective_id=0, has_side_effects=True, vmem_limit_bytes=52 * 1024 * 1024
        ),
        cost_estimate=pl.CostEstimate(
            flops=2 * tok_count * depth * width,
            bytes_accessed=2 * depth * width,
            transcendentals=0,
        ),
    )(attended, out_weight, residual, norm_gain.reshape(1, -1), jnp.asarray(signs(BLK)))


def attend_kernel(
    devices,
    query_ref,
    node_key_ref,
    node_value_ref,
    cache_key_ref,
    cache_value_ref,
    parent_ref,
    out_ref,
    keys,
    values,
    tree_keys,
    tree_values,
    acc,
    top,
    bias,
    far_send,
    far_recv,
    near_send,
    near_recv,
    keep_sem,
):
    heads, tok_count, size = query_ref.shape
    chips = devices // 2
    spread = chips // cache_key_ref.shape[0]
    length = cache_key_ref.shape[1]
    me = lax.axis_index("tensor")
    core = me % 2
    chip = me // 2
    pair = 2 * chip + 1 - core
    low = pl.ds(0, size)
    sources = (cache_key_ref, cache_value_ref, node_key_ref, node_value_ref)

    def place(a, offset, block):
        return (
            keys.at[offset, core],
            values.at[offset, core, :, low],
            tree_keys.at[block],
            tree_values.at[block, :, low],
        )[a]

    def far_copy(a, offset):
        target = (chip + offset) % chips
        return send(
            sources[a].at[target // spread],
            place(a, offset, me),
            far_send.at[a, offset],
            far_recv.at[a, offset],
            2 * target + core,
        )

    def near_copy(a, offset):
        block = 2 * ((chip + chips - offset) % chips) + core
        here = place(a, offset, block)
        src = sources[a].at[chip // spread] if isinstance(offset, int) and offset == 0 else here
        return send(src, here, near_send.at[a, offset], near_recv.at[a, offset], pair)

    def keep_copy(a):
        return pltpu.make_async_copy(
            sources[a].at[chip // spread], place(a, 0, me), keep_sem.at[a]
        )

    for a in range(4):
        keep_copy(a).start()
    values[:, :, :, size:] = jnp.ones(values.shape[:3] + (size,), jnp.bfloat16)
    tree_values[:, :, size:] = jnp.ones(tree_values.shape[:2] + (size,), jnp.bfloat16)
    greet([pair] + [2 * ((chip + o) % chips) + core for o in range(1, chips)])

    def scatter(offset, carry):
        for a in range(4):
            far_copy(a, offset).start()
        return carry

    lax.fori_loop(1, chips, scatter, 0)
    for a in range(4):
        near_copy(a, 0).start()

    index = lax.broadcasted_iota(jnp.int32, (tok_count, tok_count), 0)
    other = lax.broadcasted_iota(jnp.int32, (tok_count, tok_count), 1)
    reach = jnp.where((other == index) | (other == parent_ref[...]), 1.0, 0.0)

    def extend(step, reach):
        held = reach.astype(jnp.bfloat16)
        return jnp.minimum(jnp.dot(held, held, preferred_element_type=jnp.float32), 1.0)

    reach = lax.fori_loop(0, max(1, (tok_count - 1).bit_length()), extend, reach)
    bias[...] = jnp.where(reach > 0.5, 0.0, -1e30)

    factor = math.log2(math.e) / math.sqrt(size)

    def attend(key, value, first, masked):
        def body(head, carry):
            scores = (
                lax.dot_general(
                    query_ref[head],
                    key,
                    (((1,), (1,)), ((), ())),
                    preferred_element_type=jnp.float32,
                )
                * factor
            )
            if masked:
                scores = scores + bias[...]
            peak = jnp.max(scores, axis=1, keepdims=True)
            if not first:
                before = top[head][:, :1]
                peak = jnp.maximum(peak, before)
            weights = jnp.exp2(scores - peak).astype(jnp.bfloat16)
            mixed = jnp.dot(weights, value, preferred_element_type=jnp.float32)
            if not first:
                mixed = mixed + acc[head] * jnp.exp2(before - peak)
            if masked:
                columns = pl.ds(pl.multiple_of(head * size, size), size)
                out_ref[:, columns] = (mixed[:, :size] / mixed[:, size:]).astype(jnp.bfloat16)
            else:
                acc[head] = mixed
                top[head] = jnp.broadcast_to(peak, (tok_count, size))
            return carry

        lax.fori_loop(0, heads, body, 0, unroll=2)

    def collect(offset):
        for a in range(4):
            far_copy(a, offset).wait_recv()
            near_copy(a, offset).start()

    def chunk(j):
        for offset in (2 * j, 2 * j + 1):
            for a in range(4):
                near_copy(a, offset).wait_recv()
        span = pl.ds(2 * j, 2)
        attend(
            keys[span].reshape(4 * length, size),
            values[span].reshape(4 * length, 2 * size),
            isinstance(j, int) and j == 0,
            False,
        )

    for a in range(4):
        keep_copy(a).wait()
    collect(1)
    collect(2)
    collect(3)
    chunk(0)

    def advance(j, carry):
        collect(2 * j + 2)
        collect(2 * j + 3)
        chunk(j)
        return carry

    lax.fori_loop(1, chips // 2 - 1, advance, 0)
    chunk(chips // 2 - 1)
    attend(
        tree_keys[...].reshape(tok_count, size),
        tree_values[...].reshape(tok_count, 2 * size),
        False,
        True,
    )

    def drain(offset, carry):
        for a in range(4):
            far_copy(a, offset).wait_send()
            near_copy(a, offset).wait_send()
        return carry

    for a in range(4):
        near_copy(a, 0).wait_send()
    lax.fori_loop(1, chips, drain, 0)


def attend(devices, queries, node_keys, node_values, cache_keys, cache_values, parents):
    heads, tok_count, size = queries.shape
    chips = devices // 2
    length = cache_keys.shape[1]
    nodes = node_keys.shape[1]
    bf16, f32 = jnp.bfloat16, jnp.float32
    dma = pltpu.SemaphoreType.DMA
    vmem = pl.BlockSpec(memory_space=pltpu.VMEM)
    hbm = pl.BlockSpec(memory_space=pl.ANY)
    seen = devices * (length + nodes)
    return pl.pallas_call(
        functools.partial(attend_kernel, devices),
        out_shape=jax.ShapeDtypeStruct((tok_count, heads * size), bf16),
        in_specs=[vmem, hbm, hbm, hbm, hbm, vmem],
        out_specs=vmem,
        scratch_shapes=[
            pltpu.VMEM((chips, 2, length, size), bf16),
            pltpu.VMEM((chips, 2, length, 2 * size), bf16),
            pltpu.VMEM((devices, nodes, size), bf16),
            pltpu.VMEM((devices, nodes, 2 * size), bf16),
            pltpu.VMEM((heads, tok_count, 2 * size), f32),
            pltpu.VMEM((heads, tok_count, size), f32),
            pltpu.VMEM((tok_count, tok_count), f32),
            dma((4, chips)),
            dma((4, chips)),
            dma((4, chips)),
            dma((4, chips)),
            dma((4,)),
        ],
        compiler_params=pltpu.CompilerParams(
            collective_id=1, has_side_effects=True, vmem_limit_bytes=48 * 1024 * 1024
        ),
        cost_estimate=pl.CostEstimate(
            flops=4 * tok_count * heads * seen * size,
            bytes_accessed=4 * seen * size,
            transcendentals=tok_count * heads * seen,
        ),
    )(queries, node_keys, node_values, cache_keys, cache_values, parents.reshape(-1, 1))


def shards(
    queries,
    node_keys,
    node_values,
    cache_keys,
    cache_values,
    parents,
    out_weight,
    residual,
    norm_gain,
):
    tok_count = queries.shape[0]
    devices = lax.axis_size("tensor")
    attended = attend(
        devices,
        jnp.transpose(queries, (1, 0, 2)),
        node_keys,
        node_values,
        cache_keys,
        cache_values,
        parents,
    )
    gathered = project(devices, attended, out_weight, residual, norm_gain)
    width = out_weight.shape[1]
    return (
        gathered[:, :, :width].reshape(tok_count, width),
        gathered[:, :, width:].reshape(tok_count, width // BLK),
    )


def solution(mesh):
    in_specs = (
        P("groups", "tensor", None),
        P(None, ("groups", "tensor"), None),
        P(None, ("groups", "tensor"), None),
        P(None, ("groups", "tensor"), None),
        P(None, ("groups", "tensor"), None),
        P("groups"),
        P("tensor", None),
        P(("groups", "tensor"), None),
        P(),
    )
    out_specs = (P("groups", None), P("groups", None))
    return jax.shard_map(shards, mesh=mesh, in_specs=in_specs, out_specs=out_specs, check_vma=False)
```

```python
import functools
import math

import jax
import jax.numpy as jnp
import ml_dtypes
import numpy as np
from jax import lax
from jax.experimental import pallas as pl
from jax.experimental.pallas import tpu as pltpu
from jax.sharding import PartitionSpec as P

BLK = 128
MESH = pl.DeviceIdType.MESH


def signs(size):
    index = np.arange(size)
    both = index[:, None] & index[None, :]
    parity = np.zeros((size, size), np.int64)
    while both.any():
        parity ^= both & 1
        both = both >> 1
    return (1 - 2 * parity).astype(ml_dtypes.bfloat16)


def ring_chip(pos, chips):
    turn = chips // 2
    back = pos // turn
    return (1 - back) * (2 * pos) + back * (2 * (chips - 1 - pos) + 1)


def ring_pos(chip, chips):
    odd = chip % 2
    level = chip // 2
    return (1 - odd) * level + odd * (chips - 1 - level)


def send(src, dst, send_sem, recv_sem, target):
    return pltpu.make_async_remote_copy(
        src_ref=src,
        dst_ref=dst,
        send_sem=send_sem,
        recv_sem=recv_sem,
        device_id={"tensor": target},
        device_id_type=MESH,
    )


def greet(targets):
    barrier = pltpu.get_barrier_semaphore()
    for target in targets:
        pl.semaphore_signal(barrier, inc=1, device_id={"tensor": target}, device_id_type=MESH)
    pl.semaphore_wait(barrier, len(targets))


def project_kernel(
    devices,
    att_ref,
    weight_ref,
    residual_ref,
    gain_ref,
    table_ref,
    out_ref,
    scale_ref,
    wbuf,
    pair_out,
    pair_in,
    part,
    ring_out,
    ring_in,
    swap_out,
    swap_in,
    mine,
    state,
    packed,
    packed_scales,
    w_sem,
    pair_send,
    pair_recv,
    ring_send,
    ring_recv,
    swap_send,
    swap_recv,
    keep_sem,
    far_send,
    far_recv,
    near_send,
    near_recv,
):
    chips = devices // 2
    own, width = state.shape
    rows = 2 * own
    half_width = width // 2
    lane = half_width // 4
    tile = wbuf.shape[2]
    per = half_width // (2 * tile)
    total = 4 * per
    me = lax.axis_index("tensor")
    core = me % 2
    chip = me // 2
    pos = ring_pos(chip, chips)
    right = 2 * ring_chip((pos + 1) % chips, chips) + core
    left = 2 * ring_chip((pos + chips - 1) % chips, chips) + core
    pair = 2 * chip + 1 - core

    def fetch(step):
        phase = step // per
        side = (core + 1 + phase % 2) % 2
        column = side * half_width + ((phase // 2) * per + step % per) * tile
        return pltpu.make_async_copy(
            weight_ref.at[:, pl.ds(pl.multiple_of(column, tile), tile)],
            wbuf.at[step % 3],
            w_sem.at[step % 3],
        )

    fetch(0).start()
    fetch(1).start()
    greet((pair, left, right))

    def product(step):
        fetch(step).wait()

        @pl.when(step + 2 < total)
        def _():
            fetch(step + 2).start()

        return jnp.dot(att_ref[...], wbuf[step % 3], preferred_element_type=jnp.float32)

    def pair_copy(index):
        return send(
            pair_out.at[index], pair_in.at[index], pair_send.at[index], pair_recv.at[index], pair
        )

    def give(half):
        def body(i, carry):
            index = half * per + i
            pair_out[index] = product(2 * half * per + i).astype(jnp.bfloat16)
            pair_copy(index).start()
            return carry

        lax.fori_loop(0, per, body, 0)

    def keep(half):
        def body(i, carry):
            index = half * per + i
            own_part = product((2 * half + 1) * per + i)
            pair_copy(index).wait_recv()
            part[:, pl.ds(pl.multiple_of(index * tile, tile), tile)] = own_part + pair_in[
                index
            ].astype(jnp.float32)
            return carry

        lax.fori_loop(0, per, body, 0)

    def ring_copy(stream, step):
        return send(
            ring_out.at[stream, step],
            ring_in.at[stream, step],
            ring_send.at[stream, step],
            ring_recv.at[stream, step],
            left if stream % 2 else right,
        )

    def ring_step(stream, step, first):
        if stream % 2:
            target = (pos + 1 + step) % chips
        else:
            target = (pos + chips - 1 - step) % chips
        row = pl.multiple_of(ring_chip(target, chips) * rows, rows)
        value = part[pl.ds(row, rows), stream * lane : (stream + 1) * lane]
        if not first:
            ring_copy(stream, step - 1).wait_recv()
            value = value + ring_in[stream, step - 1].astype(jnp.float32)
        ring_out[stream, step] = value.astype(jnp.bfloat16)
        ring_copy(stream, step).start()

    give(0)
    keep(0)
    ring_step(0, 0, True)
    ring_step(1, 0, True)
    give(1)
    ring_step(0, 1, False)
    ring_step(1, 1, False)
    keep(1)
    ring_step(2, 0, True)
    ring_step(3, 0, True)

    def around(step, carry):
        for stream in (0, 1):
            ring_step(stream, step, False)
        for stream in (2, 3):
            ring_step(stream, step - 1, False)
        return carry

    lax.fori_loop(2, chips - 1, around, 0)
    for stream in (2, 3):
        ring_step(stream, chips - 2, False)
    row = pl.multiple_of(chip * rows, rows)
    for stream in range(4):
        ring_copy(stream, chips - 2).wait_recv()
        columns = slice(stream * lane, (stream + 1) * lane)
        mine[:, columns] = part[pl.ds(row, rows), columns] + ring_in[stream, chips - 2].astype(
            jnp.float32
        )
    swap_out[...] = mine[pl.ds(pl.multiple_of((1 - core) * own, own), own), :]
    swap = send(swap_out, swap_in, swap_send, swap_recv, pair)
    swap.start()
    state[:, pl.ds(pl.multiple_of(core * half_width, half_width), half_width)] = mine[
        pl.ds(pl.multiple_of(core * own, own), own), :
    ]
    swap.wait_recv()
    state[:, pl.ds(pl.multiple_of((1 - core) * half_width, half_width), half_width)] = swap_in[...]

    group = 8
    step_width = group * BLK

    def squares(i, acc):
        columns = pl.ds(pl.multiple_of(i * step_width, step_width), step_width)
        value = state[:, columns] + residual_ref[:, columns].astype(jnp.float32)
        state[:, columns] = value
        return acc + value * value

    acc = lax.fori_loop(
        0, width // step_width, squares, jnp.zeros((own, step_width), jnp.float32)
    )
    inverse = lax.rsqrt(jnp.sum(acc, axis=1, keepdims=True) / width + 1e-05)
    table = table_ref[...]
    lanes = lax.broadcasted_iota(jnp.int32, (own, width // BLK), 1)

    def rotate_group(i, scales):
        blocks = []
        for b in range(group):
            columns = pl.ds(pl.multiple_of(i * step_width + b * BLK, BLK), BLK)
            blocks.append(
                state[:, columns] * inverse * gain_ref[:, columns].astype(jnp.float32)
            )
        normed = jnp.concatenate(blocks, axis=0)
        high = normed.astype(jnp.bfloat16)
        low = (normed - high.astype(jnp.float32)).astype(jnp.bfloat16)
        rotated = (
            jnp.dot(high, table, preferred_element_type=jnp.float32)
            + jnp.dot(low, table, preferred_element_type=jnp.float32)
        ) * (1.0 / math.sqrt(BLK))
        scale = (
            (jnp.max(jnp.abs(rotated), axis=1, keepdims=True) + 1e-06)
            .astype(jnp.bfloat16)
            .astype(jnp.float32)
        )
        levels = (rotated / scale).astype(jnp.bfloat16)
        for b in range(group):
            columns = pl.ds(pl.multiple_of(i * step_width + b * BLK, BLK), BLK)
            packed[:, columns] = levels[b * own : (b + 1) * own, :]
            scales = jnp.where(lanes == i * group + b, scale[b * own : (b + 1) * own, :], scales)
        return scales

    scales = lax.fori_loop(
        0, width // step_width, rotate_group, jnp.zeros((own, width // BLK), jnp.float32)
    )
    packed_scales[...] = scales.astype(jnp.bfloat16)

    cut = width // 2

    def view(block, piece):
        if piece == 2:
            return scale_ref.at[block]
        return out_ref.at[block, :, pl.ds(piece * cut, cut)]

    def fresh(piece):
        return packed_scales if piece == 2 else packed.at[:, pl.ds(piece * cut, cut)]

    hops = chips // 2

    def owner(d, hop):
        where = (pos + hop) % chips if d else (pos + chips - hop) % chips
        return 2 * ring_chip(where, chips) + core

    def far_copy(d, hop, piece):
        block = owner(d, hop - 1)
        dst = view(block, piece)
        src = fresh(piece) if hop == 1 else dst
        at = (d * hops + hop - 1) * 3 + piece
        return send(src, dst, far_send.at[at], far_recv.at[at], left if d else right)

    def near_copy(d, hop, piece):
        block = owner(d, hop)
        dst = view(block, piece)
        src = fresh(piece) if hop == 0 else dst
        at = (d * (hops + 1) + hop) * 3 + piece
        return send(src, dst, near_send.at[at], near_recv.at[at], pair)

    def goes(d, hop, piece):
        return hop < hops or piece == d or (piece == 2 and d == 0)

    order = ((0, 0), (1, 1), (0, 1), (1, 0), (0, 2), (1, 2))
    for d, piece in order:
        far_copy(d, 1, piece).start()
    own_copies = (
        pltpu.make_async_copy(packed, out_ref.at[me], keep_sem.at[0]),
        pltpu.make_async_copy(packed_scales, scale_ref.at[me], keep_sem.at[1]),
    )
    for own_copy in own_copies:
        own_copy.start()
    for piece in range(3):
        near_copy(0, 0, piece).start()
    for hop in range(1, hops + 1):
        for d, piece in order:
            if goes(d, hop, piece):
                far_copy(d, hop, piece).wait_recv()
                if hop < hops and goes(d, hop + 1, piece):
                    far_copy(d, hop + 1, piece).start()
                near_copy(d, hop, piece).start()
    for own_copy in own_copies:
        own_copy.wait()
    for piece in range(3):
        near_copy(0, 0, piece).wait()
    for hop in range(1, hops + 1):
        for d, piece in order:
            if goes(d, hop, piece):
                far_copy(d, hop, piece).wait_send()
                near_copy(d, hop, piece).wait()
    swap.wait_send()

    def drain_pair(i, carry):
        pair_copy(i).wait_send()
        return carry

    lax.fori_loop(0, 2 * per, drain_pair, 0)

    def drain_ring(step, carry):
        for stream in range(4):
            ring_copy(stream, step).wait_send()
        return carry

    lax.fori_loop(0, chips - 1, drain_ring, 0)


def project(devices, attended, out_weight, residual, norm_gain):
    tok_count, depth = attended.shape
    width = out_weight.shape[1]
    own = residual.shape[0]
    chips = devices // 2
    hops = chips // 2
    half_width = width // 2
    lane = half_width // 4
    tile = half_width // 8
    blocks = width // BLK
    bf16, f32 = jnp.bfloat16, jnp.float32
    dma = pltpu.SemaphoreType.DMA
    vmem = pl.BlockSpec(memory_space=pltpu.VMEM)
    hbm = pl.BlockSpec(memory_space=pl.ANY)
    return pl.pallas_call(
        functools.partial(project_kernel, devices),
        out_shape=(
            jax.ShapeDtypeStruct((devices, own, width), bf16),
            jax.ShapeDtypeStruct((devices, own, blocks), bf16),
        ),
        in_specs=[vmem, hbm, vmem, vmem, vmem],
        out_specs=(hbm, hbm),
        scratch_shapes=[
            pltpu.VMEM((3, depth, tile), bf16),
            pltpu.VMEM((8, tok_count, tile), bf16),
            pltpu.VMEM((8, tok_count, tile), bf16),
            pltpu.VMEM((tok_count, half_width), f32),
            pltpu.VMEM((4, chips - 1, 2 * own, lane), bf16),
            pltpu.VMEM((4, chips - 1, 2 * own, lane), bf16),
            pltpu.VMEM((own, half_width), f32),
            pltpu.VMEM((own, half_width), f32),
            pltpu.VMEM((2 * own, half_width), f32),
            pltpu.VMEM((own, width), f32),
            pltpu.VMEM((own, width), bf16),
            pltpu.VMEM((own, blocks), bf16),
            dma((3,)),
            dma((8,)),
            dma((8,)),
            dma((4, chips - 1)),
            dma((4, chips - 1)),
            dma,
            dma,
            dma((2,)),
            dma((6 * hops,)),
            dma((6 * hops,)),
            dma((6 * (hops + 1),)),
            dma((6 * (hops + 1),)),
        ],
        compiler_params=pltpu.CompilerParams(
            collective_id=0, has_side_effects=True, vmem_limit_bytes=58 * 1024 * 1024
        ),
        cost_estimate=pl.CostEstimate(
            flops=2 * tok_count * depth * width,
            bytes_accessed=2 * depth * width,
            transcendentals=0,
        ),
    )(attended, out_weight, residual, norm_gain.reshape(1, -1), jnp.asarray(signs(BLK)))


def attend_kernel(
    devices,
    query_ref,
    node_key_ref,
    node_value_ref,
    cache_key_ref,
    cache_value_ref,
    parent_ref,
    out_ref,
    keys,
    values,
    tree_keys,
    tree_values,
    acc,
    top,
    bias,
    far_send,
    far_recv,
    near_send,
    near_recv,
    keep_sem,
):
    heads, tok_count, size = query_ref.shape
    chips = devices // 2
    spread = chips // cache_key_ref.shape[0]
    length = cache_key_ref.shape[1]
    me = lax.axis_index("tensor")
    core = me % 2
    chip = me // 2
    pair = 2 * chip + 1 - core
    low = pl.ds(0, size)
    sources = (cache_key_ref, cache_value_ref, node_key_ref, node_value_ref)

    def place(a, offset, block):
        return (
            keys.at[offset, core],
            values.at[offset, core, :, low],
            tree_keys.at[block],
            tree_values.at[block, :, low],
        )[a]

    def far_copy(a, offset):
        target = (chip + offset) % chips
        return send(
            sources[a].at[target // spread],
            place(a, offset, me),
            far_send.at[a, offset],
            far_recv.at[a, offset],
            2 * target + core,
        )

    def near_copy(a, offset):
        block = 2 * ((chip + chips - offset) % chips) + core
        here = place(a, offset, block)
        src = sources[a].at[chip // spread] if isinstance(offset, int) and offset == 0 else here
        return send(src, here, near_send.at[a, offset], near_recv.at[a, offset], pair)

    def keep_copy(a):
        return pltpu.make_async_copy(
            sources[a].at[chip // spread], place(a, 0, me), keep_sem.at[a]
        )

    for a in range(4):
        keep_copy(a).start()
    values[:, :, :, size:] = jnp.ones(values.shape[:3] + (size,), jnp.bfloat16)
    tree_values[:, :, size:] = jnp.ones(tree_values.shape[:2] + (size,), jnp.bfloat16)
    greet([pair] + [2 * ((chip + o) % chips) + core for o in range(1, chips)])

    def scatter_nodes(offset, carry):
        for a in (2, 3):
            far_copy(a, offset).start()
        return carry

    def scatter_cache(offset, carry):
        for a in (0, 1):
            far_copy(a, offset).start()
        return carry

    lax.fori_loop(1, chips, scatter_nodes, 0)
    lax.fori_loop(1, chips, scatter_cache, 0)
    for a in range(4):
        near_copy(a, 0).start()

    index = lax.broadcasted_iota(jnp.int32, (tok_count, tok_count), 0)
    other = lax.broadcasted_iota(jnp.int32, (tok_count, tok_count), 1)
    reach = jnp.where((other == index) | (other == parent_ref[...]), 1.0, 0.0)

    def extend(step, reach):
        held = reach.astype(jnp.bfloat16)
        return jnp.minimum(jnp.dot(held, held, preferred_element_type=jnp.float32), 1.0)

    reach = lax.fori_loop(0, max(1, (tok_count - 1).bit_length()), extend, reach)
    bias[...] = jnp.where(reach > 0.5, 0.0, -1e30)

    factor = math.log2(math.e) / math.sqrt(size)

    def attend(key, value, first, last):
        def body(head, carry):
            scores = (
                lax.dot_general(
                    query_ref[head],
                    key,
                    (((1,), (1,)), ((), ())),
                    preferred_element_type=jnp.float32,
                )
                * factor
            )
            if first:
                scores = scores + bias[...]
            peak = jnp.max(scores, axis=1, keepdims=True)
            if not first:
                before = top[head][:, :1]
                peak = jnp.maximum(peak, before)
            weights = jnp.exp2(scores - peak).astype(jnp.bfloat16)
            mixed = jnp.dot(weights, value, preferred_element_type=jnp.float32)
            if not first:
                mixed = mixed + acc[head] * jnp.exp2(before - peak)
            if last:
                columns = pl.ds(pl.multiple_of(head * size, size), size)
                out_ref[:, columns] = (mixed[:, :size] / mixed[:, size:]).astype(jnp.bfloat16)
            else:
                acc[head] = mixed
                top[head] = jnp.broadcast_to(peak, (tok_count, size))
            return carry

        lax.fori_loop(0, heads, body, 0, unroll=2)

    def collect(offset, which):
        for a in which:
            far_copy(a, offset).wait_recv()
            near_copy(a, offset).start()

    def settle(offset, which):
        for a in which:
            near_copy(a, offset).wait_recv()

    def chunk(j, last):
        for offset in (2 * j, 2 * j + 1):
            settle(offset, (0, 1))
        span = pl.ds(2 * j, 2)
        attend(
            keys[span].reshape(4 * length, size),
            values[span].reshape(4 * length, 2 * size),
            False,
            last,
        )

    for a in range(4):
        keep_copy(a).wait()

    def collect_nodes(offset, carry):
        collect(offset, (2, 3))
        return carry

    def settle_nodes(offset, carry):
        settle(offset, (2, 3))
        return carry

    lax.fori_loop(1, chips, collect_nodes, 0)
    lax.fori_loop(0, chips, settle_nodes, 0)
    attend(
        tree_keys[...].reshape(tok_count, size),
        tree_values[...].reshape(tok_count, 2 * size),
        True,
        False,
    )
    collect(1, (0, 1))
    chunk(0, False)

    def advance(j, carry):
        collect(2 * j, (0, 1))
        collect(2 * j + 1, (0, 1))
        chunk(j, False)
        return carry

    lax.fori_loop(1, chips // 2 - 1, advance, 0)
    collect(chips - 2, (0, 1))
    collect(chips - 1, (0, 1))
    chunk(chips // 2 - 1, True)

    def drain(offset, carry):
        for a in range(4):
            far_copy(a, offset).wait_send()
            near_copy(a, offset).wait_send()
        return carry

    for a in range(4):
        near_copy(a, 0).wait_send()
    lax.fori_loop(1, chips, drain, 0)


def attend(devices, queries, node_keys, node_values, cache_keys, cache_values, parents):
    heads, tok_count, size = queries.shape
    chips = devices // 2
    length = cache_keys.shape[1]
    nodes = node_keys.shape[1]
    bf16, f32 = jnp.bfloat16, jnp.float32
    dma = pltpu.SemaphoreType.DMA
    vmem = pl.BlockSpec(memory_space=pltpu.VMEM)
    hbm = pl.BlockSpec(memory_space=pl.ANY)
    seen = devices * (length + nodes)
    return pl.pallas_call(
        functools.partial(attend_kernel, devices),
        out_shape=jax.ShapeDtypeStruct((tok_count, heads * size), bf16),
        in_specs=[vmem, hbm, hbm, hbm, hbm, vmem],
        out_specs=vmem,
        scratch_shapes=[
            pltpu.VMEM((chips, 2, length, size), bf16),
            pltpu.VMEM((chips, 2, length, 2 * size), bf16),
            pltpu.VMEM((devices, nodes, size), bf16),
            pltpu.VMEM((devices, nodes, 2 * size), bf16),
            pltpu.VMEM((heads, tok_count, 2 * size), f32),
            pltpu.VMEM((heads, tok_count, size), f32),
            pltpu.VMEM((tok_count, tok_count), f32),
            dma((4, chips)),
            dma((4, chips)),
            dma((4, chips)),
            dma((4, chips)),
            dma((4,)),
        ],
        compiler_params=pltpu.CompilerParams(
            collective_id=1, has_side_effects=True, vmem_limit_bytes=60 * 1024 * 1024
        ),
        cost_estimate=pl.CostEstimate(
            flops=4 * tok_count * heads * seen * size,
            bytes_accessed=4 * seen * size,
            transcendentals=tok_count * heads * seen,
        ),
    )(queries, node_keys, node_values, cache_keys, cache_values, parents.reshape(-1, 1))


def shards(
    queries,
    node_keys,
    node_values,
    cache_keys,
    cache_values,
    parents,
    out_weight,
    residual,
    norm_gain,
):
    tok_count = queries.shape[0]
    devices = lax.axis_size("tensor")
    attended = attend(
        devices,
        jnp.transpose(queries, (1, 0, 2)),
        node_keys,
        node_values,
        cache_keys,
        cache_values,
        parents,
    )
    levels, scales = project(devices, attended, out_weight, residual, norm_gain)
    width = out_weight.shape[1]
    return (levels.reshape(tok_count, width), scales.reshape(tok_count, width // BLK))


def solution(mesh):
    in_specs = (
        P("groups", "tensor", None),
        P(None, ("groups", "tensor"), None),
        P(None, ("groups", "tensor"), None),
        P(None, ("groups", "tensor"), None),
        P(None, ("groups", "tensor"), None),
        P("groups"),
        P("tensor", None),
        P(("groups", "tensor"), None),
        P(),
    )
    out_specs = (P("groups", None), P("groups", None))
    return jax.shard_map(shards, mesh=mesh, in_specs=in_specs, out_specs=out_specs, check_vma=False)
```

```python
import functools
import math

import jax
import jax.numpy as jnp
import ml_dtypes
import numpy as np
from jax import lax
from jax.experimental import pallas as pl
from jax.experimental.pallas import tpu as pltpu
from jax.sharding import PartitionSpec as P

BLK = 128
MESH = pl.DeviceIdType.MESH


def signs(size):
    index = np.arange(size)
    both = index[:, None] & index[None, :]
    parity = np.zeros((size, size), np.int64)
    while both.any():
        parity ^= both & 1
        both = both >> 1
    return (1 - 2 * parity).astype(ml_dtypes.bfloat16)


def ring_chip(pos, chips):
    turn = chips // 2
    back = pos // turn
    return (1 - back) * (2 * pos) + back * (2 * (chips - 1 - pos) + 1)


def ring_pos(chip, chips):
    odd = chip % 2
    level = chip // 2
    return (1 - odd) * level + odd * (chips - 1 - level)


def send(src, dst, send_sem, recv_sem, target):
    return pltpu.make_async_remote_copy(
        src_ref=src,
        dst_ref=dst,
        send_sem=send_sem,
        recv_sem=recv_sem,
        device_id={"tensor": target},
        device_id_type=MESH,
    )


def greet(targets):
    barrier = pltpu.get_barrier_semaphore()
    for target in targets:
        pl.semaphore_signal(barrier, inc=1, device_id={"tensor": target}, device_id_type=MESH)
    pl.semaphore_wait(barrier, len(targets))


def project_kernel(
    devices,
    att_ref,
    weight_ref,
    residual_ref,
    gain_ref,
    table_ref,
    out_ref,
    scale_ref,
    wbuf,
    pair_out,
    pair_in,
    part,
    ring_out,
    ring_in,
    swap_out,
    swap_in,
    mine,
    state,
    packed,
    packed_scales,
    w_sem,
    pair_send,
    pair_recv,
    ring_send,
    ring_recv,
    swap_send,
    swap_recv,
    keep_sem,
    far_send,
    far_recv,
    near_send,
    near_recv,
):
    chips = devices // 2
    own, width = state.shape
    rows = 2 * own
    half_width = width // 2
    lane = half_width // 4
    tile = wbuf.shape[2]
    per = half_width // (2 * tile)
    total = 4 * per
    me = lax.axis_index("tensor")
    core = me % 2
    chip = me // 2
    pos = ring_pos(chip, chips)
    right = 2 * ring_chip((pos + 1) % chips, chips) + core
    left = 2 * ring_chip((pos + chips - 1) % chips, chips) + core
    pair = 2 * chip + 1 - core

    def fetch(step):
        phase = step // per
        side = (core + 1 + phase % 2) % 2
        column = side * half_width + ((phase // 2) * per + step % per) * tile
        return pltpu.make_async_copy(
            weight_ref.at[:, pl.ds(pl.multiple_of(column, tile), tile)],
            wbuf.at[step % 3],
            w_sem.at[step % 3],
        )

    fetch(0).start()
    fetch(1).start()
    greet((pair, left, right))

    def product(step):
        fetch(step).wait()

        @pl.when(step + 2 < total)
        def _():
            fetch(step + 2).start()

        return jnp.dot(att_ref[...], wbuf[step % 3], preferred_element_type=jnp.float32)

    def pair_copy(index):
        return send(
            pair_out.at[index], pair_in.at[index], pair_send.at[index], pair_recv.at[index], pair
        )

    def give(half):
        def body(i, carry):
            index = half * per + i
            pair_out[index] = product(2 * half * per + i).astype(jnp.bfloat16)
            pair_copy(index).start()
            return carry

        lax.fori_loop(0, per, body, 0)

    def keep(half):
        def body(i, carry):
            index = half * per + i
            own_part = product((2 * half + 1) * per + i)
            pair_copy(index).wait_recv()
            part[:, pl.ds(pl.multiple_of(index * tile, tile), tile)] = own_part + pair_in[
                index
            ].astype(jnp.float32)
            return carry

        lax.fori_loop(0, per, body, 0)

    def ring_copy(stream, step):
        return send(
            ring_out.at[stream, step],
            ring_in.at[stream, step],
            ring_send.at[stream, step],
            ring_recv.at[stream, step],
            left if stream % 2 else right,
        )

    def ring_step(stream, step, first):
        if stream % 2:
            target = (pos + 1 + step) % chips
        else:
            target = (pos + chips - 1 - step) % chips
        row = pl.multiple_of(ring_chip(target, chips) * rows, rows)
        value = part[pl.ds(row, rows), stream * lane : (stream + 1) * lane]
        if not first:
            ring_copy(stream, step - 1).wait_recv()
            value = value + ring_in[stream, step - 1].astype(jnp.float32)
        ring_out[stream, step] = value.astype(jnp.bfloat16)
        ring_copy(stream, step).start()

    give(0)
    keep(0)
    ring_step(0, 0, True)
    ring_step(1, 0, True)
    give(1)
    ring_step(0, 1, False)
    ring_step(1, 1, False)
    keep(1)
    ring_step(2, 0, True)
    ring_step(3, 0, True)

    def around(step, carry):
        for stream in (0, 1):
            ring_step(stream, step, False)
        for stream in (2, 3):
            ring_step(stream, step - 1, False)
        return carry

    lax.fori_loop(2, chips - 1, around, 0)
    for stream in (2, 3):
        ring_step(stream, chips - 2, False)
    row = pl.multiple_of(chip * rows, rows)
    for stream in range(4):
        ring_copy(stream, chips - 2).wait_recv()
        columns = slice(stream * lane, (stream + 1) * lane)
        mine[:, columns] = part[pl.ds(row, rows), columns] + ring_in[stream, chips - 2].astype(
            jnp.float32
        )
    swap_out[...] = mine[pl.ds(pl.multiple_of((1 - core) * own, own), own), :]
    swap = send(swap_out, swap_in, swap_send, swap_recv, pair)
    swap.start()
    state[:, pl.ds(pl.multiple_of(core * half_width, half_width), half_width)] = mine[
        pl.ds(pl.multiple_of(core * own, own), own), :
    ]
    swap.wait_recv()
    state[:, pl.ds(pl.multiple_of((1 - core) * half_width, half_width), half_width)] = swap_in[...]

    group = 8
    step_width = group * BLK

    def squares(i, acc):
        columns = pl.ds(pl.multiple_of(i * step_width, step_width), step_width)
        value = state[:, columns] + residual_ref[:, columns].astype(jnp.float32)
        state[:, columns] = value
        return acc + value * value

    acc = lax.fori_loop(
        0, width // step_width, squares, jnp.zeros((own, step_width), jnp.float32)
    )
    inverse = lax.rsqrt(jnp.sum(acc, axis=1, keepdims=True) / width + 1e-05)
    table = table_ref[...]
    lanes = lax.broadcasted_iota(jnp.int32, (own, width // BLK), 1)

    def rotate_group(i, scales):
        blocks = []
        for b in range(group):
            columns = pl.ds(pl.multiple_of(i * step_width + b * BLK, BLK), BLK)
            blocks.append(
                state[:, columns] * inverse * gain_ref[:, columns].astype(jnp.float32)
            )
        normed = jnp.concatenate(blocks, axis=0)
        high = normed.astype(jnp.bfloat16)
        low = (normed - high.astype(jnp.float32)).astype(jnp.bfloat16)
        rotated = (
            jnp.dot(high, table, preferred_element_type=jnp.float32)
            + jnp.dot(low, table, preferred_element_type=jnp.float32)
        ) * (1.0 / math.sqrt(BLK))
        scale = (
            (jnp.max(jnp.abs(rotated), axis=1, keepdims=True) + 1e-06)
            .astype(jnp.bfloat16)
            .astype(jnp.float32)
        )
        levels = (rotated / scale).astype(jnp.bfloat16)
        for b in range(group):
            columns = pl.ds(pl.multiple_of(i * step_width + b * BLK, BLK), BLK)
            packed[:, columns] = levels[b * own : (b + 1) * own, :]
            scales = jnp.where(lanes == i * group + b, scale[b * own : (b + 1) * own, :], scales)
        return scales

    scales = lax.fori_loop(
        0, width // step_width, rotate_group, jnp.zeros((own, width // BLK), jnp.float32)
    )
    packed_scales[...] = scales.astype(jnp.bfloat16)

    cut = width // 2

    def view(block, piece):
        if piece == 2:
            return scale_ref.at[block]
        return out_ref.at[block, :, pl.ds(piece * cut, cut)]

    def fresh(piece):
        return packed_scales if piece == 2 else packed.at[:, pl.ds(piece * cut, cut)]

    hops = chips // 2

    def owner(d, hop):
        where = (pos + hop) % chips if d else (pos + chips - hop) % chips
        return 2 * ring_chip(where, chips) + core

    def far_copy(d, hop, piece):
        block = owner(d, hop - 1)
        dst = view(block, piece)
        src = fresh(piece) if hop == 1 else dst
        at = (d * hops + hop - 1) * 3 + piece
        return send(src, dst, far_send.at[at], far_recv.at[at], left if d else right)

    def near_copy(d, hop, piece):
        block = owner(d, hop)
        dst = view(block, piece)
        src = fresh(piece) if hop == 0 else dst
        at = (d * (hops + 1) + hop) * 3 + piece
        return send(src, dst, near_send.at[at], near_recv.at[at], pair)

    def goes(d, hop, piece):
        return hop < hops or piece == d or (piece == 2 and d == 0)

    order = ((0, 0), (1, 1), (0, 1), (1, 0), (0, 2), (1, 2))
    for d, piece in order:
        far_copy(d, 1, piece).start()
    own_copies = (
        pltpu.make_async_copy(packed, out_ref.at[me], keep_sem.at[0]),
        pltpu.make_async_copy(packed_scales, scale_ref.at[me], keep_sem.at[1]),
    )
    for own_copy in own_copies:
        own_copy.start()
    for piece in range(3):
        near_copy(0, 0, piece).start()
    for hop in range(1, hops + 1):
        for d, piece in order:
            if goes(d, hop, piece):
                far_copy(d, hop, piece).wait_recv()
                if hop < hops and goes(d, hop + 1, piece):
                    far_copy(d, hop + 1, piece).start()
                near_copy(d, hop, piece).start()
    for own_copy in own_copies:
        own_copy.wait()
    for piece in range(3):
        near_copy(0, 0, piece).wait()
    for hop in range(1, hops + 1):
        for d, piece in order:
            if goes(d, hop, piece):
                far_copy(d, hop, piece).wait_send()
                near_copy(d, hop, piece).wait()
    swap.wait_send()

    def drain_pair(i, carry):
        pair_copy(i).wait_send()
        return carry

    lax.fori_loop(0, 2 * per, drain_pair, 0)

    def drain_ring(step, carry):
        for stream in range(4):
            ring_copy(stream, step).wait_send()
        return carry

    lax.fori_loop(0, chips - 1, drain_ring, 0)


def project(devices, attended, out_weight, residual, norm_gain):
    tok_count, depth = attended.shape
    width = out_weight.shape[1]
    own = residual.shape[0]
    chips = devices // 2
    hops = chips // 2
    half_width = width // 2
    lane = half_width // 4
    tile = half_width // 8
    blocks = width // BLK
    bf16, f32 = jnp.bfloat16, jnp.float32
    dma = pltpu.SemaphoreType.DMA
    vmem = pl.BlockSpec(memory_space=pltpu.VMEM)
    hbm = pl.BlockSpec(memory_space=pl.ANY)
    return pl.pallas_call(
        functools.partial(project_kernel, devices),
        out_shape=(
            jax.ShapeDtypeStruct((devices, own, width), bf16),
            jax.ShapeDtypeStruct((devices, own, blocks), bf16),
        ),
        in_specs=[vmem, hbm, vmem, vmem, vmem],
        out_specs=(hbm, hbm),
        scratch_shapes=[
            pltpu.VMEM((3, depth, tile), bf16),
            pltpu.VMEM((8, tok_count, tile), bf16),
            pltpu.VMEM((8, tok_count, tile), bf16),
            pltpu.VMEM((tok_count, half_width), f32),
            pltpu.VMEM((4, chips - 1, 2 * own, lane), bf16),
            pltpu.VMEM((4, chips - 1, 2 * own, lane), bf16),
            pltpu.VMEM((own, half_width), f32),
            pltpu.VMEM((own, half_width), f32),
            pltpu.VMEM((2 * own, half_width), f32),
            pltpu.VMEM((own, width), f32),
            pltpu.VMEM((own, width), bf16),
            pltpu.VMEM((own, blocks), bf16),
            dma((3,)),
            dma((8,)),
            dma((8,)),
            dma((4, chips - 1)),
            dma((4, chips - 1)),
            dma,
            dma,
            dma((2,)),
            dma((6 * hops,)),
            dma((6 * hops,)),
            dma((6 * (hops + 1),)),
            dma((6 * (hops + 1),)),
        ],
        compiler_params=pltpu.CompilerParams(
            collective_id=0, has_side_effects=True, vmem_limit_bytes=58 * 1024 * 1024
        ),
        cost_estimate=pl.CostEstimate(
            flops=2 * tok_count * depth * width,
            bytes_accessed=2 * depth * width,
            transcendentals=0,
        ),
    )(attended, out_weight, residual, norm_gain.reshape(1, -1), jnp.asarray(signs(BLK)))


def attend_kernel(
    devices,
    query_ref,
    node_key_ref,
    node_value_ref,
    cache_key_ref,
    cache_value_ref,
    parent_ref,
    out_ref,
    keys,
    values,
    tree_keys,
    tree_values,
    acc,
    top,
    bias,
    far_send,
    far_recv,
    near_send,
    near_recv,
    keep_sem,
):
    heads, tok_count, size = query_ref.shape
    chips = devices // 2
    spread = chips // cache_key_ref.shape[0]
    length = cache_key_ref.shape[1]
    me = lax.axis_index("tensor")
    core = me % 2
    chip = me // 2
    pair = 2 * chip + 1 - core
    low = pl.ds(0, size)
    sources = (cache_key_ref, cache_value_ref, node_key_ref, node_value_ref)

    def place(a, offset, block):
        return (
            keys.at[offset, core],
            values.at[offset, core, :, low],
            tree_keys.at[block],
            tree_values.at[block, :, low],
        )[a]

    def far_copy(a, offset):
        target = (chip + offset) % chips
        return send(
            sources[a].at[target // spread],
            place(a, offset, me),
            far_send.at[a, offset],
            far_recv.at[a, offset],
            2 * target + core,
        )

    def near_copy(a, offset):
        block = 2 * ((chip + chips - offset) % chips) + core
        here = place(a, offset, block)
        src = sources[a].at[chip // spread] if isinstance(offset, int) and offset == 0 else here
        return send(src, here, near_send.at[a, offset], near_recv.at[a, offset], pair)

    def keep_copy(a):
        return pltpu.make_async_copy(
            sources[a].at[chip // spread], place(a, 0, me), keep_sem.at[a]
        )

    for a in range(4):
        keep_copy(a).start()
    values[:, :, :, size:] = jnp.ones(values.shape[:3] + (size,), jnp.bfloat16)
    tree_values[:, :, size:] = jnp.ones(tree_values.shape[:2] + (size,), jnp.bfloat16)
    greet([pair] + [2 * ((chip + o) % chips) + core for o in range(1, chips)])

    def scatter_nodes(offset, carry):
        for a in (2, 3):
            far_copy(a, offset).start()
        return carry

    def scatter_cache(offset, carry):
        for a in (0, 1):
            far_copy(a, offset).start()
        return carry

    lax.fori_loop(1, chips, scatter_nodes, 0)
    lax.fori_loop(1, chips, scatter_cache, 0)
    for a in range(4):
        near_copy(a, 0).start()

    index = lax.broadcasted_iota(jnp.int32, (tok_count, tok_count), 0)
    other = lax.broadcasted_iota(jnp.int32, (tok_count, tok_count), 1)
    reach = jnp.where((other == index) | (other == parent_ref[...]), 1.0, 0.0)

    def extend(step, reach):
        held = reach.astype(jnp.bfloat16)
        return jnp.minimum(jnp.dot(held, held, preferred_element_type=jnp.float32), 1.0)

    reach = lax.fori_loop(0, max(1, (tok_count - 1).bit_length()), extend, reach)
    bias[...] = jnp.where(reach > 0.5, 0.0, -1e30)

    factor = math.log2(math.e) / math.sqrt(size)

    def attend(key, value, first, last):
        def body(head, carry):
            scores = (
                lax.dot_general(
                    query_ref[head],
                    key,
                    (((1,), (1,)), ((), ())),
                    preferred_element_type=jnp.float32,
                )
                * factor
            )
            if first:
                scores = scores + bias[...]
            peak = jnp.max(scores, axis=1, keepdims=True)
            if not first:
                before = top[head][:, :1]
                peak = jnp.maximum(peak, before)
            weights = jnp.exp2(scores - peak).astype(jnp.bfloat16)
            mixed = jnp.dot(weights, value, preferred_element_type=jnp.float32)
            if not first:
                mixed = mixed + acc[head] * jnp.exp2(before - peak)
            if last:
                columns = pl.ds(pl.multiple_of(head * size, size), size)
                out_ref[:, columns] = (mixed[:, :size] / mixed[:, size:]).astype(jnp.bfloat16)
            else:
                acc[head] = mixed
                top[head] = jnp.broadcast_to(peak, (tok_count, size))
            return carry

        lax.fori_loop(0, heads, body, 0, unroll=4)

    def collect(offset, which):
        for a in which:
            far_copy(a, offset).wait_recv()
            near_copy(a, offset).start()

    def settle(offset, which):
        for a in which:
            near_copy(a, offset).wait_recv()

    def chunk(j, last):
        for offset in (2 * j, 2 * j + 1):
            settle(offset, (0, 1))
        span = pl.ds(2 * j, 2)
        attend(
            keys[span].reshape(4 * length, size),
            values[span].reshape(4 * length, 2 * size),
            False,
            last,
        )

    for a in range(4):
        keep_copy(a).wait()

    def collect_nodes(offset, carry):
        collect(offset, (2, 3))
        return carry

    def settle_nodes(offset, carry):
        settle(offset, (2, 3))
        return carry

    lax.fori_loop(1, chips, collect_nodes, 0)
    lax.fori_loop(0, chips, settle_nodes, 0)
    attend(
        tree_keys[...].reshape(tok_count, size),
        tree_values[...].reshape(tok_count, 2 * size),
        True,
        False,
    )
    collect(1, (0, 1))
    collect(2, (0, 1))
    collect(3, (0, 1))
    chunk(0, False)

    def advance(j, carry):
        collect(2 * j + 2, (0, 1))
        collect(2 * j + 3, (0, 1))
        chunk(j, False)
        return carry

    lax.fori_loop(1, chips // 2 - 1, advance, 0)
    chunk(chips // 2 - 1, True)

    def drain(offset, carry):
        for a in range(4):
            far_copy(a, offset).wait_send()
            near_copy(a, offset).wait_send()
        return carry

    for a in range(4):
        near_copy(a, 0).wait_send()
    lax.fori_loop(1, chips, drain, 0)


def attend(devices, queries, node_keys, node_values, cache_keys, cache_values, parents):
    heads, tok_count, size = queries.shape
    chips = devices // 2
    length = cache_keys.shape[1]
    nodes = node_keys.shape[1]
    bf16, f32 = jnp.bfloat16, jnp.float32
    dma = pltpu.SemaphoreType.DMA
    vmem = pl.BlockSpec(memory_space=pltpu.VMEM)
    hbm = pl.BlockSpec(memory_space=pl.ANY)
    seen = devices * (length + nodes)
    return pl.pallas_call(
        functools.partial(attend_kernel, devices),
        out_shape=jax.ShapeDtypeStruct((tok_count, heads * size), bf16),
        in_specs=[vmem, hbm, hbm, hbm, hbm, vmem],
        out_specs=vmem,
        scratch_shapes=[
            pltpu.VMEM((chips, 2, length, size), bf16),
            pltpu.VMEM((chips, 2, length, 2 * size), bf16),
            pltpu.VMEM((devices, nodes, size), bf16),
            pltpu.VMEM((devices, nodes, 2 * size), bf16),
            pltpu.VMEM((heads, tok_count, 2 * size), f32),
            pltpu.VMEM((heads, tok_count, size), f32),
            pltpu.VMEM((tok_count, tok_count), f32),
            dma((4, chips)),
            dma((4, chips)),
            dma((4, chips)),
            dma((4, chips)),
            dma((4,)),
        ],
        compiler_params=pltpu.CompilerParams(
            collective_id=1, has_side_effects=True, vmem_limit_bytes=60 * 1024 * 1024
        ),
        cost_estimate=pl.CostEstimate(
            flops=4 * tok_count * heads * seen * size,
            bytes_accessed=4 * seen * size,
            transcendentals=tok_count * heads * seen,
        ),
    )(queries, node_keys, node_values, cache_keys, cache_values, parents.reshape(-1, 1))


def shards(
    queries,
    node_keys,
    node_values,
    cache_keys,
    cache_values,
    parents,
    out_weight,
    residual,
    norm_gain,
):
    tok_count = queries.shape[0]
    devices = lax.axis_size("tensor")
    attended = attend(
        devices,
        jnp.transpose(queries, (1, 0, 2)),
        node_keys,
        node_values,
        cache_keys,
        cache_values,
        parents,
    )
    levels, scales = project(devices, attended, out_weight, residual, norm_gain)
    width = out_weight.shape[1]
    return (levels.reshape(tok_count, width), scales.reshape(tok_count, width // BLK))


def solution(mesh):
    in_specs = (
        P("groups", "tensor", None),
        P(None, ("groups", "tensor"), None),
        P(None, ("groups", "tensor"), None),
        P(None, ("groups", "tensor"), None),
        P(None, ("groups", "tensor"), None),
        P("groups"),
        P("tensor", None),
        P(("groups", "tensor"), None),
        P(),
    )
    out_specs = (P("groups", None), P("groups", None))
    return jax.shard_map(shards, mesh=mesh, in_specs=in_specs, out_specs=out_specs, check_vma=False)
```
